512 devices in a mesh: frame: 16 (over z_hi, x, core), tensor: 8 (over y), dp: 4 (over z_lo).
Axes of the slice: x: 4, y: 8, z: 8 (z_hi: 2, z_lo: 4; z = z_hi * 4 + z_lo), core: 2. Of those that a mesh axis runs over, the one named last changes fastest.
Arguments:
- queries: bfloat16 [12, 16, 256, 2048], P('dp', 'frame', None, 'tensor'), may hold values from -8 to 8
- keys: bfloat16 [12, 16, 256, 2048], P('dp', 'frame', None, 'tensor'), may hold values from -8 to 8
- values: bfloat16 [12, 16, 256, 2048], P('dp', 'frame', None, 'tensor'), may hold values from -6 to 6
- out_grad: bfloat16 [12, 16, 256, 2048], P('dp', 'frame', None, 'tensor'), may hold values from -6 to 6
- out_proj: bfloat16 [2048, 2048], P('tensor'), may hold values from -0.125 to 0.125
Outputs:
- grad_queries: bfloat16 [12, 16, 256, 2048], P('dp', 'frame', None, 'tensor')
- grad_keys: bfloat16 [12, 16, 256, 2048], P('dp', 'frame', None, 'tensor')
- grad_values: bfloat16 [12, 16, 256, 2048], P('dp', 'frame', None, 'tensor')
- grad_proj: bfloat16 [2048, 2048], P('tensor')
The draws below stay inside these ranges and needn't reach their ends.
All inputs are finite; a program needn't handle non-finite values.
Results may differ from the reference program's by a relative error of at most 0.0075.
Values may be sent and summed in bfloat16 or wider, within the bound.
No kernel may reach another device: no remote copies, remote signals or barrier semaphores. Data moves between devices by JAX's collectives and lax.ppermute only.
A program may use at most 64 MiB of HBM per device.

```python
import math
import jax
import jax.numpy as jnp
from jax import lax

D = 2048
HEADS = 16
HEAD = 128
PATCHES = 256
FRAMES = 16
CLIPS = 12


def draw_queries(key, part):
    shape = (CLIPS, FRAMES, PATCHES, HEADS, HEAD)
    key = jax.random.fold_in(key, 1)
    result = jnp.clip(jax.random.normal(key, shape, jnp.float32), -8.0, 8.0)
    return result.reshape(CLIPS, FRAMES, PATCHES, HEADS * HEAD).astype(jnp.bfloat16)


def draw_keys(key, part):
    shape = (CLIPS, FRAMES, PATCHES, HEADS, HEAD)
    key = jax.random.fold_in(key, 2)
    result = jnp.clip(jax.random.normal(key, shape, jnp.float32), -8.0, 8.0)
    return result.reshape(CLIPS, FRAMES, PATCHES, HEADS * HEAD).astype(jnp.bfloat16)


def block_scale(stream_key, shape, cuts, low, top_value):
    def one(dim, parts):
        heights = jax.random.uniform(jax.random.fold_in(jax.random.fold_in(stream_key, 6), dim), (parts,), jnp.float32, low / len(cuts), top_value / len(cuts))
        return jnp.repeat(jnp.exp(heights), shape[dim] // parts).reshape((-1,) + (1,) * (len(shape) - dim - 1))

    level = one(*cuts[0])
    for cut in cuts[1:]:
        level = level * one(*cut)
    return level


def bell_draw(stream_key, dims, spread, limit, cuts=(), held_as=jnp.bfloat16):
    level = block_scale(stream_key, dims, cuts, -0.22, 0.18) if cuts else 1.0
    values = jax.random.normal(stream_key, dims, jnp.float32) * spread * level
    return jnp.minimum(jnp.maximum(values, -limit), limit).astype(held_as)


def setup_inputs(seed: int = 0) -> dict:
    seeds = jax.random.split(jax.random.key(seed), 6)
    queries = draw_queries(jax.random.fold_in(seeds[5], 71), 0)
    keys = draw_keys(jax.random.fold_in(seeds[5], 71), 0)
    values = bell_draw(seeds[2], (CLIPS, FRAMES, PATCHES, HEADS * HEAD), 1.0, 6.0, ((0, 4), (1, 16), (3, 8)))
    out_grad = bell_draw(seeds[3], (CLIPS, FRAMES, PATCHES, D), 1.0, 6.0, ((0, 4), (1, 16), (3, 8)))
    out_proj = bell_draw(seeds[4], (HEADS * HEAD, D), (HEADS * HEAD) ** -0.5, 0.125, ((0, 8),))
    return {"queries": queries, "keys": keys, "values": values, "out_grad": out_grad, "out_proj": out_proj}


def attend(queries, keys, values, grad_attended):
    lead = queries.shape[:-3]
    frames, patches, width = queries.shape[-3:]
    count = width // HEAD
    scale = 1.0 / math.sqrt(HEAD)

    def split(array):
        return array.reshape(lead + (frames, patches, count, HEAD)).astype(jnp.float32)
    query_f, key_f, value_f, grad_f = (split(queries), split(keys), split(values), split(grad_attended))
    rows = lax.broadcasted_iota(jnp.int32, (frames, frames), 0)
    cols = lax.broadcasted_iota(jnp.int32, (frames, frames), 1)
    causal = cols <= rows
    scores = jnp.einsum('...ipne,...jpne->...pnij', query_f, key_f) * scale
    scores = jnp.where(causal, scores, -1e+30)
    top = lax.optimization_barrier(jnp.max(scores, axis=-1, keepdims=True))
    expon = jnp.where(causal, jnp.exp(scores - top), 0.0)
    probs = expon / lax.optimization_barrier(jnp.sum(expon, axis=-1, keepdims=True))
    weights = lax.optimization_barrier(probs.astype(jnp.bfloat16)).astype(jnp.float32)
    attended = jnp.einsum('...pnij,...jpne->...ipne', weights, value_f).astype(jnp.bfloat16)
    grad_probs = jnp.einsum('...ipne,...jpne->...pnij', grad_f, value_f)
    grad_values = jnp.einsum('...pnij,...ipne->...jpne', weights, grad_f).astype(jnp.bfloat16)
    row_total = lax.optimization_barrier(jnp.sum(probs * grad_probs, axis=-1, keepdims=True))
    grad_scores = (probs * (grad_probs - row_total) * scale).astype(jnp.bfloat16)
    grad_scores = lax.optimization_barrier(grad_scores).astype(jnp.float32)
    grad_queries = jnp.einsum('...pnij,...jpne->...ipne', grad_scores, key_f).astype(jnp.bfloat16)
    grad_keys = jnp.einsum('...pnij,...ipne->...jpne', grad_scores, query_f).astype(jnp.bfloat16)
    shape = lead + (frames, patches, width)
    return (attended.reshape(shape), grad_queries.reshape(shape), grad_keys.reshape(shape), grad_values.reshape(shape))

def reference(queries, keys, values, out_grad, out_proj):
    width = queries.shape[-1]
    factor = 1.0 / math.sqrt(CLIPS * FRAMES * PATCHES)

    def one_clip(total, pieces):
        query_c, key_c, value_c, grad_c = pieces
        flat = grad_c.reshape(-1, D)
        grad_att = lax.dot_general(flat, out_proj, (((1,), (1,)), ((), ())), preferred_element_type=jnp.float32)
        grad_att = grad_att.astype(jnp.bfloat16).reshape(query_c.shape)
        attended, grad_q, grad_k, grad_v = attend(query_c, key_c, value_c, grad_att)
        term = lax.dot_general(attended.reshape(-1, width), flat, (((0,), (0,)), ((), ())), preferred_element_type=jnp.float32)
        return (total + term, (grad_q, grad_k, grad_v))
    start = jnp.zeros((width, D), jnp.float32)
    total, outs = lax.scan(one_clip, start, (queries, keys, values, out_grad))
    grad_proj = (total * factor).astype(jnp.bfloat16)
    return (outs[0], outs[1], outs[2], grad_proj)
```

```python
import functools
import math

import jax
import jax.numpy as jnp
from jax import lax
from jax.experimental import pallas as pl
from jax.experimental.pallas import tpu as pltpu
from jax.sharding import Mesh, PartitionSpec as P

HEAD = 128
SCALE = 1.0 / math.sqrt(HEAD)
GROUP = 16
FRAME = ("zh", "x", "core")
BF16 = jnp.bfloat16
F32 = jnp.float32


def dot(a, b, dims):
    return lax.dot_general(a, b, (dims, ((), ())), preferred_element_type=F32)


def dot_nt(a, b):
    return dot(a, b, ((1,), (1,)))


def dot_nn(a, b):
    return dot(a, b, ((1,), (0,)))


def dot_tn(a, b):
    return dot(a, b, ((0,), (0,)))


def causal_mask(rows):
    r = lax.broadcasted_iota(jnp.int32, (rows, rows), 0)
    c = lax.broadcasted_iota(jnp.int32, (rows, rows), 1)
    return ((r % GROUP) == (c % GROUP)) & (c // GROUP <= r // GROUP)


def softmax(q, k):
    mask = causal_mask(q.shape[0])
    scores = jnp.where(mask, dot_nt(q, k) * SCALE, -1e30)
    top = jnp.max(scores, axis=1, keepdims=True)
    expon = jnp.where(mask, jnp.exp(scores - top), 0.0)
    return expon / jnp.sum(expon, axis=1, keepdims=True)


def forward_kernel(qkv_ref, att_ref):
    frames = qkv_ref.shape[0]
    rows = frames * GROUP
    q, k, v = (qkv_ref[:, j].reshape(rows, HEAD) for j in range(3))
    weights = softmax(q, k).astype(BF16)
    att_ref[...] = dot_nn(weights, v).astype(BF16).reshape(frames, GROUP, HEAD)


def backward_kernel(qkv_ref, g_ref, out_ref):
    frames = qkv_ref.shape[0]
    rows = frames * GROUP
    q, k, v = (qkv_ref[:, j].reshape(rows, HEAD) for j in range(3))
    g = g_ref[...].reshape(rows, HEAD)
    probs = softmax(q, k)
    weights = probs.astype(BF16)
    grad_probs = dot_nt(g, v)
    total = jnp.sum(probs * grad_probs, axis=1, keepdims=True)
    grad_scores = (probs * (grad_probs - total) * SCALE).astype(BF16)
    shape = (frames, GROUP, HEAD)
    out_ref[:, 0] = dot_nn(grad_scores, k).astype(BF16).reshape(shape)
    out_ref[:, 1] = dot_tn(grad_scores, q).astype(BF16).reshape(shape)
    out_ref[:, 2] = dot_tn(weights, g).astype(BF16).reshape(shape)


def project_kernel(grad_ref, w_ref, att_ref, g_ref, term_ref, acc_ref):
    step = pl.program_id(0)
    block = grad_ref[0]
    part = dot_nt(block, w_ref[...])

    @pl.when(step == 0)
    def _():
        acc_ref[...] = part

    @pl.when(step > 0)
    def _():
        acc_ref[...] += part

    term_ref[...] = dot_tn(att_ref[...], block).astype(BF16)

    @pl.when(step == pl.num_programs(0) - 1)
    def _():
        g_ref[...] = acc_ref[...].astype(BF16)


def forward(qkv):
    frames, _, items, width = qkv.shape
    return pl.pallas_call(
        forward_kernel,
        grid=(items // GROUP, width // HEAD),
        in_specs=[pl.BlockSpec((frames, 3, GROUP, HEAD), lambda i, h: (0, 0, i, h))],
        out_specs=pl.BlockSpec((frames, GROUP, HEAD), lambda i, h: (0, i, h)),
        out_shape=jax.ShapeDtypeStruct((frames, items, width), BF16),
        cost_estimate=pl.CostEstimate(flops=400_000_000, bytes_accessed=1_600_000, transcendentals=400_000),
        name="attention_forward",
    )(qkv)


def backward(qkv, g):
    frames, _, items, width = qkv.shape
    return pl.pallas_call(
        backward_kernel,
        grid=(items // GROUP, width // HEAD),
        in_specs=[
            pl.BlockSpec((frames, 3, GROUP, HEAD), lambda i, h: (0, 0, i, h)),
            pl.BlockSpec((frames, GROUP, HEAD), lambda i, h: (0, i, h)),
        ],
        out_specs=pl.BlockSpec((frames, 3, GROUP, HEAD), lambda i, h: (0, 0, i, h)),
        out_shape=jax.ShapeDtypeStruct(qkv.shape, BF16),
        cost_estimate=pl.CostEstimate(flops=1_000_000_000, bytes_accessed=3_000_000, transcendentals=400_000),
        name="attention_backward",
    )(qkv, g)


def project(grad_all, w, att):
    parts, tokens, width = grad_all.shape
    return pl.pallas_call(
        project_kernel,
        grid=(parts,),
        in_specs=[
            pl.BlockSpec((1, tokens, width), lambda s: (s, 0, 0)),
            pl.BlockSpec((width, width), lambda s: (0, s)),
            pl.BlockSpec((tokens, width), lambda s: (0, 0)),
        ],
        out_specs=[
            pl.BlockSpec((tokens, width), lambda s: (0, 0)),
            pl.BlockSpec((width, width), lambda s: (0, s)),
        ],
        out_shape=[
            jax.ShapeDtypeStruct((tokens, width), BF16),
            jax.ShapeDtypeStruct((width, parts * width), BF16),
        ],
        scratch_shapes=[pltpu.VMEM((tokens, width), F32)],
        compiler_params=pltpu.CompilerParams(vmem_limit_bytes=16 * 1024 * 1024),
        cost_estimate=pl.CostEstimate(flops=1_600_000_000, bytes_accessed=6_000_000, transcendentals=0),
        name="projections",
    )(grad_all, w, att)


def exchange(x, axes):
    return lax.all_to_all(x, axes, 0, 0, tiled=True)


def scatter_sum(x, axes, size):
    parts = exchange(x.reshape(size, -1, x.shape[-1]), axes)
    return jnp.sum(parts.astype(F32), axis=0)


def gather(x, axes, size):
    return exchange(jnp.broadcast_to(x[None], (size,) + x.shape), axes).reshape(-1, x.shape[-1])


def local(queries, keys, values, out_grad, out_proj):
    clips, _, patches, width = queries.shape
    frames = lax.axis_size(FRAME)
    tokens = clips * patches
    items = tokens // frames
    factor = 1.0 / math.sqrt(tokens * frames * lax.axis_size("dp"))

    grad_own = exchange(out_grad.reshape(frames, items, width), FRAME)
    grad_all = lax.all_gather(grad_own.reshape(tokens, width), "tensor")
    qkv = jnp.stack([a.reshape(frames, items, width) for a in (queries, keys, values)], axis=1)
    qkv = exchange(qkv, FRAME)
    att = forward(qkv)
    g, term = project(grad_all, out_proj, att.reshape(tokens, width))
    grads = backward(qkv, g.reshape(frames, items, width))

    total = scatter_sum(term, "core", 2).astype(BF16)
    total = scatter_sum(total, "x", 4).astype(BF16)
    total = (scatter_sum(total, ("zh", "dp"), 8) * factor).astype(BF16)
    total = gather(total, ("zh", "dp"), 8)
    total = gather(total, "x", 4)
    grad_proj = gather(total, "core", 2)

    home = exchange(grads, FRAME)
    return tuple(home[:, j].reshape(queries.shape) for j in range(3)) + (grad_proj,)


def solution(mesh):
    fine = Mesh(mesh.devices.reshape(2, 4, 2, 8, 4), ("zh", "x", "core", "tensor", "dp"))
    spec = P("dp", FRAME, None, "tensor")
    return jax.shard_map(
        local,
        mesh=fine,
        in_specs=(spec, spec, spec, spec, P("tensor", None)),
        out_specs=(spec, spec, spec, P("tensor", None)),
        check_vma=False,
    )
```

```python
import functools
import math

import jax
import jax.numpy as jnp
from jax import lax
from jax.experimental import pallas as pl
from jax.experimental.pallas import tpu as pltpu
from jax.sharding import Mesh, PartitionSpec as P

HEAD = 128
SCALE = 1.0 / math.sqrt(HEAD)
MASKED = -1e30
GROUP = 16
STEP = 2
NEAR = ("x", "core")
BF16 = jnp.bfloat16
F32 = jnp.float32
SMEM = pl.BlockSpec(memory_space=pltpu.SMEM)
PARAMS = pltpu.CompilerParams(vmem_limit_bytes=32 * 1024 * 1024)


def dot(a, b, dims):
    return lax.dot_general(a, b, (dims, ((), ())), preferred_element_type=F32)


def dot_nt(a, b):
    return dot(a, b, ((1,), (1,)))


def dot_nn(a, b):
    return dot(a, b, ((1,), (0,)))


def dot_tn(a, b):
    return dot(a, b, ((0,), (0,)))


def masks(rows, crossing):
    key = lax.broadcasted_iota(jnp.int32, (rows, rows), 0)
    query = lax.broadcasted_iota(jnp.int32, (rows, rows), 1)
    own = (key % GROUP == query % GROUP) & (key // GROUP <= query // GROUP)
    cross = key % GROUP == query % GROUP + jnp.where(crossing, 0, GROUP)
    return own, cross


def scores_of(mask, keys, queries):
    return jnp.where(mask, dot_nt(keys, queries) * SCALE, MASKED)


def head_slices(ref):
    return [slice(h * HEAD, (h + 1) * HEAD) for h in range(ref.shape[-1] // HEAD)]


def take(ref, j, cols):
    return ref[:, j, :, cols].reshape(-1, HEAD)


def softmax(q, k, k_cross, own_mask, cross_mask):
    s_own, s_cross = scores_of(own_mask, k, q), scores_of(cross_mask, k_cross, q)
    top = jnp.maximum(jnp.max(s_own, axis=0, keepdims=True), jnp.max(s_cross, axis=0, keepdims=True))
    e_own, e_cross = jnp.exp(s_own - top), jnp.exp(s_cross - top)
    total = jnp.sum(e_own, axis=0, keepdims=True) + jnp.sum(e_cross, axis=0, keepdims=True)
    return e_own / total, e_cross / total, top, total


def attend_kernel(side_ref, q_ref, kv_ref, recv_ref, att_ref):
    frames = q_ref.shape[0]
    own_mask, cross_mask = masks(frames * GROUP, side_ref[0] == 1)
    for cols in head_slices(q_ref):
        (k, v), (k_cross, v_cross) = ([take(ref, j, cols) for j in range(2)] for ref in (kv_ref, recv_ref))
        q = q_ref[:, :, cols].reshape(-1, HEAD)
        p_own, p_cross, _, _ = softmax(q, k, k_cross, own_mask, cross_mask)
        att = dot_tn(p_own.astype(BF16), v) + dot_tn(p_cross.astype(BF16), v_cross)
        att_ref[:, :, cols] = att.astype(BF16).reshape(frames, GROUP, HEAD)


def query_kernel(side_ref, q_ref, kv_ref, recv_ref, g_ref, out_ref, stats_ref):
    frames = q_ref.shape[0]
    own_mask, cross_mask = masks(frames * GROUP, side_ref[0] == 1)
    for h, cols in enumerate(head_slices(q_ref)):
        (k, v), (k_cross, v_cross) = ([take(ref, j, cols) for j in range(2)] for ref in (kv_ref, recv_ref))
        q = q_ref[:, :, cols].reshape(-1, HEAD)
        p_own, p_cross, top, total = softmax(q, k, k_cross, own_mask, cross_mask)
        g = g_ref[:, :, cols].reshape(-1, HEAD)
        gp_own, gp_cross = dot_nt(v, g), dot_nt(v_cross, g)
        row = jnp.sum(p_own * gp_own, axis=0, keepdims=True) + jnp.sum(p_cross * gp_cross, axis=0, keepdims=True)
        ds_own = (p_own * (gp_own - row) * SCALE).astype(BF16)
        ds_cross = (p_cross * (gp_cross - row) * SCALE).astype(BF16)
        grad = dot_tn(ds_own, k) + dot_tn(ds_cross, k_cross)
        out_ref[:, :, cols] = grad.astype(BF16).reshape(frames, GROUP, HEAD)
        for j, stat in enumerate((top, total, row)):
            stats_ref[0, 3 * h + j : 3 * h + j + 1] = stat


def key_kernel(side_ref, q_ref, kv_ref, q_recv_ref, g_ref, g_recv_ref, stats_ref, stats_recv_ref, gq_ref, out_ref):
    frames = q_ref.shape[0]
    shape = (frames, GROUP, HEAD)
    own_mask, cross_mask = masks(frames * GROUP, side_ref[0] == 0)
    out_ref[:, 0] = gq_ref[...]
    for h, cols in enumerate(head_slices(q_ref)):
        k, v = take(kv_ref, 0, cols), take(kv_ref, 1, cols)
        grad_k, grad_v = 0.0, 0.0
        for mask, q, g, stats in (
            (own_mask, q_ref[:, :, cols], g_ref[:, :, cols], stats_ref),
            (cross_mask, q_recv_ref[:, :, cols], g_recv_ref[:, :, cols], stats_recv_ref),
        ):
            top, total, row = (stats[0, 3 * h + j : 3 * h + j + 1] for j in range(3))
            q, g = q.reshape(-1, HEAD), g.reshape(-1, HEAD)
            probs = jnp.where(mask, jnp.exp(scores_of(mask, k, q) - top) / total, 0.0)
            ds = (probs * (dot_nt(v, g) - row) * SCALE).astype(BF16)
            grad_k = grad_k + dot_nn(ds, q)
            grad_v = grad_v + dot_nn(probs.astype(BF16), g)
        out_ref[:, 1, :, cols] = grad_k.astype(BF16).reshape(shape)
        out_ref[:, 2, :, cols] = grad_v.astype(BF16).reshape(shape)


def project_kernel(offsets, place_ref, w_ref, att_ref, *refs):
    blocks, (g_ref, term_ref) = refs[:-2], refs[-2:]
    width = w_ref.shape[0]
    parts = w_ref.shape[1] // width
    half = att_ref.shape[0] // 2

    def columns(offset):
        owner = lax.rem(place_ref[0] + offset + parts, parts)
        return pl.ds(pl.multiple_of(owner * width, width), width)

    acc = 0.0
    for offset, ref in zip(offsets, blocks[:-2]):
        acc = acc + dot_nt(ref[...], w_ref[:, columns(offset)])
        term_ref[:, columns(offset)] = dot_tn(att_ref[...], ref[...]).astype(BF16)
    last = columns(parts // 2)
    low, high = blocks[-2][...], blocks[-1][...]
    g_ref[:half] = (acc[:half] + dot_nt(low, w_ref[:, last])).astype(BF16)
    g_ref[half:] = (acc[half:] + dot_nt(high, w_ref[:, last])).astype(BF16)
    term_ref[:, last] = (dot_tn(att_ref[:half], low) + dot_tn(att_ref[half:], high)).astype(BF16)


def per_group(kernel, name, flops, side, args, outs, vmem=32):
    items = args[0].shape[-2]

    def spec(a):
        if a.dtype == F32:
            return pl.BlockSpec((1,) + a.shape[1:], lambda i: (i, 0, 0))
        block = a.shape[:-2] + (GROUP, a.shape[-1])
        lead = (0,) * (len(a.shape) - 2)
        return pl.BlockSpec(block, lambda i: lead + (i, 0))

    return pl.pallas_call(
        kernel,
        grid=(items // GROUP,),
        in_specs=[SMEM] + [spec(a) for a in args],
        out_specs=[spec(a) for a in outs],
        out_shape=[jax.ShapeDtypeStruct(a.shape, a.dtype) for a in outs],
        compiler_params=pltpu.CompilerParams(vmem_limit_bytes=vmem * 1024 * 1024),
        cost_estimate=pl.CostEstimate(flops=flops, bytes_accessed=4_000_000, transcendentals=400_000),
        name=name,
    )(side, *args)


def project(blocks, offsets, w, att):
    tokens, width = att.shape
    vmem = pl.BlockSpec(memory_space=pltpu.VMEM)
    return pl.pallas_call(
        functools.partial(project_kernel, offsets),
        in_specs=[pl.BlockSpec(memory_space=pltpu.SMEM)] + [vmem] * (2 + len(blocks)),
        out_specs=[vmem, vmem],
        out_shape=[
            jax.ShapeDtypeStruct((tokens, width), BF16),
            jax.ShapeDtypeStruct(w.shape, BF16),
        ],
        compiler_params=pltpu.CompilerParams(vmem_limit_bytes=24 * 1024 * 1024),
        cost_estimate=pl.CostEstimate(flops=1_600_000_000, bytes_accessed=6_000_000, transcendentals=0),
        name="projections",
    )(lax.axis_index("tensor").reshape(1), w, att, *blocks)


def exchange(x, axes):
    return lax.all_to_all(x, axes, 0, 0, tiled=True)


def scatter_sum(x, axes):
    parts = exchange(x.reshape(lax.axis_size(axes), -1, x.shape[-1]), axes)
    return jnp.sum(parts.astype(F32), axis=0)


def shift(x, axis, by):
    size = lax.axis_size(axis)
    return lax.ppermute(x, axis, [(i, (i + by) % size) for i in range(size)])


def ring(x):
    size = lax.axis_size("tensor")
    half = x.shape[0] // 2
    blocks, offsets, up, down = [x], [0], x, x
    for step in range(1, size // 2):
        up, down = shift(up, "tensor", 1), shift(down, "tensor", -1)
        blocks += [up, down]
        offsets += [-step, step]
    blocks += [shift(up[:half], "tensor", 1), shift(down[half:], "tensor", -1)]
    return blocks, offsets


def gather(x, axes):
    copies = jnp.broadcast_to(x[None], (lax.axis_size(axes),) + x.shape)
    return exchange(copies, axes).reshape(-1, x.shape[-1])


def local(queries, keys, values, out_grad, out_proj):
    clips, _, patches, width = queries.shape
    near = lax.axis_size(NEAR)
    tokens = clips * patches
    items = tokens // near
    factor = 1.0 / math.sqrt(tokens * near * lax.axis_size("zh") * lax.axis_size("dp"))
    side = lax.axis_index("zh").astype(jnp.int32).reshape(1)
    queries, keys, values, out_grad = (a.reshape(near, items, width) for a in (queries, keys, values, out_grad))

    grad_own = exchange(out_grad, NEAR).reshape(tokens, width)
    qkv, grad_own = lax.optimization_barrier((jnp.stack([queries, keys, values], axis=1), grad_own))
    qkv = exchange(qkv, NEAR)
    q, kv = qkv[:, 0], qkv[:, 1:]
    kv_recv = lax.ppermute(kv, "zh", [(0, 1)])
    blocks, offsets = ring(grad_own)
    like = jax.ShapeDtypeStruct(q.shape, BF16)
    q_recv = lax.ppermute(q, "zh", [(1, 0)])
    (att,) = per_group(attend_kernel, "attend", 400_000_000, side, [q, kv, kv_recv], [like])
    g, term = project(blocks, offsets, out_proj, att.reshape(tokens, width))
    g, term, q_recv = lax.optimization_barrier((g, term, q_recv))
    g = g.reshape(att.shape)
    g_recv = lax.ppermute(g, "zh", [(1, 0)])

    stats = jax.ShapeDtypeStruct((items // GROUP, 8, near * GROUP), F32)
    grad_q, stats = per_group(query_kernel, "grad_queries", 700_000_000, side, [q, kv, kv_recv, g], [like, stats])

    total = scatter_sum(term, "x").astype(BF16)
    total = scatter_sum(total, "core").astype(BF16)
    total, g_recv, grad_q, stats = lax.optimization_barrier((total, g_recv, grad_q, stats))
    stats_recv = lax.ppermute(stats, "zh", [(1, 0)])
    total = (scatter_sum(total, ("zh", "dp")) * factor).astype(BF16)
    total, stats_recv = lax.optimization_barrier((total, stats_recv))
    args = [q, kv, q_recv, g, g_recv, stats, stats_recv, grad_q]
    grads = jax.ShapeDtypeStruct((near, 3, items, width), BF16)
    (grads,) = per_group(key_kernel, "grad_keys_values", 1_000_000_000, side, args, [grads], 60)
    total = gather(total, ("zh", "dp"))
    total, grads = lax.optimization_barrier((total, grads))
    home = exchange(grads, NEAR)
    total, home = lax.optimization_barrier((total, home))
    total = gather(total, "x")
    grad_proj = gather(total, "core").reshape(lax.axis_size("core"), lax.axis_size("x"), -1, total.shape[-1])
    grad_proj = jnp.swapaxes(grad_proj, 0, 1).reshape(out_proj.shape)
    return tuple(home[:, j].reshape(clips, 1, patches, width) for j in range(3)) + (grad_proj,)


def solution(mesh):
    fine = Mesh(mesh.devices.reshape(2, 4, 2, 8, 4), ("zh", "x", "core", "tensor", "dp"))
    spec = P("dp", ("zh", "x", "core"), None, "tensor")
    return jax.shard_map(
        local,
        mesh=fine,
        in_specs=(spec, spec, spec, spec, P("tensor", None)),
        out_specs=(spec, spec, spec, P("tensor", None)),
        check_vma=False,
    )
```

```python
import functools
import math

import jax
import jax.numpy as jnp
from jax import lax
from jax.experimental import pallas as pl
from jax.experimental.pallas import tpu as pltpu
from jax.sharding import Mesh, PartitionSpec as P

HEAD = 128
SCALE = 1.0 / math.sqrt(HEAD)
MASKED = -1e30
GROUP = 16
STEP = 2
NEAR = ("x", "core")
BF16 = jnp.bfloat16
F32 = jnp.float32
SMEM = pl.BlockSpec(memory_space=pltpu.SMEM)
PARAMS = pltpu.CompilerParams(vmem_limit_bytes=32 * 1024 * 1024)


def dot(a, b, dims):
    return lax.dot_general(a, b, (dims, ((), ())), preferred_element_type=F32)


def dot_nt(a, b):
    return dot(a, b, ((1,), (1,)))


def dot_nn(a, b):
    return dot(a, b, ((1,), (0,)))


def dot_tn(a, b):
    return dot(a, b, ((0,), (0,)))


def masks(rows, crossing):
    key = lax.broadcasted_iota(jnp.int32, (rows, rows), 0)
    query = lax.broadcasted_iota(jnp.int32, (rows, rows), 1)
    own = (key % GROUP == query % GROUP) & (key // GROUP <= query // GROUP)
    cross = key % GROUP == query % GROUP + jnp.where(crossing, 0, GROUP)
    return own, cross


def scores_of(mask, keys, queries):
    return jnp.where(mask, dot_nt(keys, queries) * SCALE, MASKED)


def head_slices(ref):
    return [slice(h * HEAD, (h + 1) * HEAD) for h in range(ref.shape[-1] // HEAD)]


def take(ref, j, cols):
    return ref[:, j, :, cols].reshape(-1, HEAD)


def softmax(q, k, k_cross, own_mask, cross_mask):
    s_own, s_cross = scores_of(own_mask, k, q), scores_of(cross_mask, k_cross, q)
    top = jnp.maximum(jnp.max(s_own, axis=0, keepdims=True), jnp.max(s_cross, axis=0, keepdims=True))
    e_own, e_cross = jnp.exp(s_own - top), jnp.exp(s_cross - top)
    total = jnp.sum(e_own, axis=0, keepdims=True) + jnp.sum(e_cross, axis=0, keepdims=True)
    return e_own / total, e_cross / total, top, total


def attend_kernel(side_ref, q_ref, kv_ref, recv_ref, att_ref):
    frames = q_ref.shape[0]
    own_mask, cross_mask = masks(frames * GROUP, side_ref[0] == 1)
    for cols in head_slices(q_ref):
        (k, v), (k_cross, v_cross) = ([take(ref, j, cols) for j in range(2)] for ref in (kv_ref, recv_ref))
        q = q_ref[:, :, cols].reshape(-1, HEAD)
        p_own, p_cross, _, _ = softmax(q, k, k_cross, own_mask, cross_mask)
        att = dot_tn(p_own.astype(BF16), v) + dot_tn(p_cross.astype(BF16), v_cross)
        att_ref[:, :, cols] = att.astype(BF16).reshape(frames, GROUP, HEAD)


def query_kernel(side_ref, q_ref, kv_ref, recv_ref, g_ref, out_ref, stats_ref):
    frames = q_ref.shape[0]
    own_mask, cross_mask = masks(frames * GROUP, side_ref[0] == 1)
    for h, cols in enumerate(head_slices(q_ref)):
        (k, v), (k_cross, v_cross) = ([take(ref, j, cols) for j in range(2)] for ref in (kv_ref, recv_ref))
        q = q_ref[:, :, cols].reshape(-1, HEAD)
        p_own, p_cross, top, total = softmax(q, k, k_cross, own_mask, cross_mask)
        g = g_ref[:, :, cols].reshape(-1, HEAD)
        gp_own, gp_cross = dot_nt(v, g), dot_nt(v_cross, g)
        row = jnp.sum(p_own * gp_own, axis=0, keepdims=True) + jnp.sum(p_cross * gp_cross, axis=0, keepdims=True)
        ds_own = (p_own * (gp_own - row) * SCALE).astype(BF16)
        ds_cross = (p_cross * (gp_cross - row) * SCALE).astype(BF16)
        grad = dot_tn(ds_own, k) + dot_tn(ds_cross, k_cross)
        out_ref[:, :, cols] = grad.astype(BF16).reshape(frames, GROUP, HEAD)
        for j, stat in enumerate((top, total, row)):
            stats_ref[0, 3 * h + j : 3 * h + j + 1] = stat


def key_kernel(side_ref, q_ref, kv_ref, q_recv_ref, g_ref, g_recv_ref, stats_ref, stats_recv_ref, gq_ref, out_ref):
    frames = q_ref.shape[0]
    shape = (frames, GROUP, HEAD)
    own_mask, cross_mask = masks(frames * GROUP, side_ref[0] == 0)
    out_ref[:, 0] = gq_ref[...]
    for h, cols in enumerate(head_slices(q_ref)):
        k, v = take(kv_ref, 0, cols), take(kv_ref, 1, cols)
        grad_k, grad_v = 0.0, 0.0
        for mask, q, g, stats in (
            (own_mask, q_ref[:, :, cols], g_ref[:, :, cols], stats_ref),
            (cross_mask, q_recv_ref[:, :, cols], g_recv_ref[:, :, cols], stats_recv_ref),
        ):
            top, total, row = (stats[0, 3 * h + j : 3 * h + j + 1] for j in range(3))
            q, g = q.reshape(-1, HEAD), g.reshape(-1, HEAD)
            probs = jnp.where(mask, jnp.exp(scores_of(mask, k, q) - top) / total, 0.0)
            ds = (probs * (dot_nt(v, g) - row) * SCALE).astype(BF16)
            grad_k = grad_k + dot_nn(ds, q)
            grad_v = grad_v + dot_nn(probs.astype(BF16), g)
        out_ref[:, 1, :, cols] = grad_k.astype(BF16).reshape(shape)
        out_ref[:, 2, :, cols] = grad_v.astype(BF16).reshape(shape)


def project_kernel(offsets, place_ref, w_ref, att_ref, *refs):
    blocks, (acc_ref, term_ref) = refs[:-2], refs[-2:]
    width = w_ref.shape[0]
    parts = w_ref.shape[1] // width
    acc = 0.0
    for offset, ref in zip(offsets, blocks):
        owner = lax.rem(place_ref[0] + offset + parts, parts)
        cols = pl.ds(pl.multiple_of(owner * width, width), width)
        acc = acc + dot_nt(ref[...], w_ref[:, cols])
        term_ref[:, cols] = dot_tn(att_ref[...], ref[...]).astype(BF16)
    acc_ref[...] = acc


def finish_kernel(place_ref, w_ref, att_ref, acc_ref, low_ref, high_ref, _, g_ref, term_ref):
    half = low_ref.shape[0]
    low, high = low_ref[...], high_ref[...]
    g_ref[:half] = (acc_ref[:half] + dot_nt(low, w_ref[...])).astype(BF16)
    g_ref[half:] = (acc_ref[half:] + dot_nt(high, w_ref[...])).astype(BF16)
    term_ref[...] = (dot_tn(att_ref[:half], low) + dot_tn(att_ref[half:], high)).astype(BF16)


def per_group(kernel, name, flops, side, args, outs, vmem=32, out_specs=None):
    items = args[0].shape[-2]

    def spec(a):
        if a.dtype == F32:
            return pl.BlockSpec((1,) + a.shape[1:], lambda i: (i, 0, 0))
        block = a.shape[:-2] + (GROUP, a.shape[-1])
        lead = (0,) * (len(a.shape) - 2)
        return pl.BlockSpec(block, lambda i: lead + (i, 0))

    return pl.pallas_call(
        kernel,
        grid=(items // GROUP,),
        in_specs=[SMEM] + [spec(a) for a in args],
        out_specs=out_specs or [spec(a) for a in outs],
        out_shape=[jax.ShapeDtypeStruct(a.shape, a.dtype) for a in outs],
        compiler_params=pltpu.CompilerParams(vmem_limit_bytes=vmem * 1024 * 1024),
        cost_estimate=pl.CostEstimate(flops=flops, bytes_accessed=4_000_000, transcendentals=400_000),
        name=name,
    )(side, *args)


def project(blocks, offsets, w, att):
    tokens, width = att.shape
    parts = w.shape[1] // width
    place = lax.axis_index("tensor")
    vmem = pl.BlockSpec(memory_space=pltpu.VMEM)
    acc, term = pl.pallas_call(
        functools.partial(project_kernel, offsets),
        in_specs=[SMEM] + [vmem] * len(blocks),
        out_specs=[vmem, vmem],
        out_shape=[jax.ShapeDtypeStruct((tokens, width), F32), jax.ShapeDtypeStruct(w.shape, BF16)],
        compiler_params=PARAMS,
        cost_estimate=pl.CostEstimate(flops=1_400_000_000, bytes_accessed=6_000_000, transcendentals=0),
        name="projections",
    )(place.reshape(1), w, att, *blocks[:-2])
    strip = pl.BlockSpec((width, width), lambda i, owner: (0, owner[0]))

    def whole(a):
        return pl.BlockSpec(a.shape, lambda i, owner: (0, 0))

    owner = lax.rem(place + parts // 2, parts).reshape(1)
    args = [w, att, acc, *blocks[-2:], term]
    return pl.pallas_call(
        finish_kernel,
        grid_spec=pltpu.PrefetchScalarGridSpec(
            num_scalar_prefetch=1,
            grid=(1,),
            in_specs=[strip] + [whole(a) for a in args[1:-1]] + [pl.BlockSpec(memory_space=pl.ANY)],
            out_specs=[whole(att), strip],
        ),
        out_shape=[jax.ShapeDtypeStruct(att.shape, BF16), jax.ShapeDtypeStruct(term.shape, BF16)],
        input_output_aliases={len(args): 1},
        compiler_params=PARAMS,
        cost_estimate=pl.CostEstimate(flops=200_000_000, bytes_accessed=3_000_000, transcendentals=0),
        name="last_projections",
    )(owner, *args)


def exchange(x, axes):
    return lax.all_to_all(x, axes, 0, 0, tiled=True)


def scatter_sum(x, axes):
    parts = exchange(x.reshape(lax.axis_size(axes), -1, x.shape[-1]), axes)
    return jnp.sum(parts.astype(F32), axis=0)


def shift(x, axis, by):
    size = lax.axis_size(axis)
    return lax.ppermute(x, axis, [(i, (i + by) % size) for i in range(size)])


def ring(x):
    size = lax.axis_size("tensor")
    half = x.shape[0] // 2
    blocks, offsets, up, down = [x], [0], x, x
    for step in range(1, size // 2):
        up, down = shift(up, "tensor", 1), shift(down, "tensor", -1)
        blocks += [up, down]
        offsets += [-step, step]
    blocks += [shift(up[:half], "tensor", 1), shift(down[half:], "tensor", -1)]
    return blocks, offsets


def gather(x, axes):
    copies = jnp.broadcast_to(x[None], (lax.axis_size(axes),) + x.shape)
    return exchange(copies, axes).reshape(-1, x.shape[-1])


def local(queries, keys, values, out_grad, out_proj):
    clips, _, patches, width = queries.shape
    near = lax.axis_size(NEAR)
    tokens = clips * patches
    items = tokens // near
    factor = 1.0 / math.sqrt(tokens * near * lax.axis_size("zh") * lax.axis_size("dp"))
    side = lax.axis_index("zh").astype(jnp.int32).reshape(1)
    queries, keys, values, out_grad = (a.reshape(near, items, width) for a in (queries, keys, values, out_grad))

    grad_own = exchange(out_grad, NEAR).reshape(tokens, width)
    qkv, grad_own = lax.optimization_barrier((jnp.stack([queries, keys, values], axis=1), grad_own))
    qkv = exchange(qkv, NEAR)
    q, kv = qkv[:, 0], qkv[:, 1:]
    kv_recv = lax.ppermute(kv, "zh", [(0, 1)])
    blocks, offsets = ring(grad_own)
    like = jax.ShapeDtypeStruct(q.shape, BF16)
    q_recv = lax.ppermute(q, "zh", [(1, 0)])
    (att,) = per_group(attend_kernel, "attend", 400_000_000, side, [q, kv, kv_recv], [like])
    g, term = project(blocks, offsets, out_proj, att.reshape(tokens, width))
    g, term, q_recv = lax.optimization_barrier((g, term, q_recv))
    g = g.reshape(att.shape)
    g_recv = lax.ppermute(g, "zh", [(1, 0)])

    stats = jax.ShapeDtypeStruct((items // GROUP, 8, near * GROUP), F32)
    grad_q, stats = per_group(query_kernel, "grad_queries", 700_000_000, side, [q, kv, kv_recv, g], [like, stats])

    total = scatter_sum(term, "x").astype(BF16)
    total = scatter_sum(total, "core").astype(BF16)
    total, g_recv, grad_q, stats = lax.optimization_barrier((total, g_recv, grad_q, stats))
    stats_recv = lax.ppermute(stats, "zh", [(1, 0)])
    total = (scatter_sum(total, ("zh", "dp")) * factor).astype(BF16)
    total, stats_recv = lax.optimization_barrier((total, stats_recv))
    args = [q, kv, q_recv, g, g_recv, stats, stats_recv, grad_q]
    groups, share = items // GROUP, out_proj.size // (near * GROUP * width)
    grads = jax.ShapeDtypeStruct((near, 3 * groups + share, GROUP, width), BF16)
    block = pl.BlockSpec((near, 3, GROUP, width), lambda i: (0, i, 0, 0))
    (grads,) = per_group(key_kernel, "grad_keys_values", 1_000_000_000, side, args, [grads], 60, [block])
    total = gather(total, ("zh", "dp"))
    total, grads = lax.optimization_barrier((total, grads))
    copies = jnp.broadcast_to(total.reshape(1, share, GROUP, width), (near, share, GROUP, width))
    home = exchange(lax.dynamic_update_slice(grads, copies, (0, 3 * groups, 0, 0)), NEAR)
    grad_proj = home[:, 3 * groups :].reshape(out_proj.shape)
    grads = home[:, : 3 * groups].reshape(near, groups, 3, GROUP, width)
    return tuple(grads[:, :, j].reshape(clips, 1, patches, width) for j in range(3)) + (grad_proj,)


def solution(mesh):
    fine = Mesh(mesh.devices.reshape(2, 4, 2, 8, 4), ("zh", "x", "core", "tensor", "dp"))
    spec = P("dp", ("zh", "x", "core"), None, "tensor")
    return jax.shard_map(
        local,
        mesh=fine,
        in_specs=(spec, spec, spec, spec, P("tensor", None)),
        out_specs=(spec, spec, spec, P("tensor", None)),
        check_vma=False,
    )
```

```python
import functools
import math

import jax
import jax.numpy as jnp
from jax import lax
from jax.experimental import pallas as pl
from jax.experimental.pallas import tpu as pltpu
from jax.sharding import Mesh, PartitionSpec as P

HEAD = 128
SCALE = 1.0 / math.sqrt(HEAD)
MASKED = -1e30
GROUP = 16
STEP_GROUPS = 2
NEAR = ("x", "core")
BF16 = jnp.bfloat16
F32 = jnp.float32
SMEM = pl.BlockSpec(memory_space=pltpu.SMEM)
PARAMS = pltpu.CompilerParams(vmem_limit_bytes=16 * 1024 * 1024)


def dot(a, b, dims):
    return lax.dot_general(a, b, (dims, ((), ())), preferred_element_type=F32)


def dot_nt(a, b):
    return dot(a, b, ((1,), (1,)))


def dot_nn(a, b):
    return dot(a, b, ((1,), (0,)))


def dot_tn(a, b):
    return dot(a, b, ((0,), (0,)))


def masks(rows, crossing):
    key = lax.broadcasted_iota(jnp.int32, (rows, rows), 0)
    query = lax.broadcasted_iota(jnp.int32, (rows, rows), 1)
    own = (key % GROUP == query % GROUP) & (key // GROUP <= query // GROUP)
    cross = key % GROUP == query % GROUP + jnp.where(crossing, 0, GROUP)
    return own, cross


def scores_of(mask, keys, queries):
    return jnp.where(mask, dot_nt(keys, queries) * SCALE, MASKED)


def pieces(ref):
    for i in range(STEP_GROUPS):
        for h in range(ref.shape[-1] // HEAD):
            yield i, h, slice(i * GROUP, (i + 1) * GROUP), slice(h * HEAD, (h + 1) * HEAD)


def take(ref, j, rows, cols):
    return ref[:, j, rows, cols].reshape(-1, HEAD)


def softmax(q, k, k_cross, own_mask, cross_mask):
    s_own, s_cross = scores_of(own_mask, k, q), scores_of(cross_mask, k_cross, q)
    top = jnp.maximum(jnp.max(s_own, axis=0, keepdims=True), jnp.max(s_cross, axis=0, keepdims=True))
    e_own, e_cross = jnp.exp(s_own - top), jnp.exp(s_cross - top)
    total = jnp.sum(e_own, axis=0, keepdims=True) + jnp.sum(e_cross, axis=0, keepdims=True)
    return e_own / total, e_cross / total, top, total


def attend_kernel(side_ref, q_ref, kv_ref, recv_ref, att_ref):
    frames = q_ref.shape[0]
    own_mask, cross_mask = masks(frames * GROUP, side_ref[0] == 1)
    for _, _, rows, cols in pieces(q_ref):
        (k, v), (k_cross, v_cross) = ([take(ref, j, rows, cols) for j in range(2)] for ref in (kv_ref, recv_ref))
        q = q_ref[:, rows, cols].reshape(-1, HEAD)
        p_own, p_cross, _, _ = softmax(q, k, k_cross, own_mask, cross_mask)
        att = dot_tn(p_own.astype(BF16), v) + dot_tn(p_cross.astype(BF16), v_cross)
        att_ref[:, rows, cols] = att.astype(BF16).reshape(frames, GROUP, HEAD)


def query_kernel(side_ref, q_ref, kv_ref, recv_ref, g_ref, out_ref, stats_ref):
    frames = q_ref.shape[0]
    own_mask, cross_mask = masks(frames * GROUP, side_ref[0] == 1)
    for i, h, rows, cols in pieces(q_ref):
        (k, v), (k_cross, v_cross) = ([take(ref, j, rows, cols) for j in range(2)] for ref in (kv_ref, recv_ref))
        q = q_ref[:, rows, cols].reshape(-1, HEAD)
        p_own, p_cross, top, total = softmax(q, k, k_cross, own_mask, cross_mask)
        g = g_ref[:, rows, cols].reshape(-1, HEAD)
        gp_own, gp_cross = dot_nt(v, g), dot_nt(v_cross, g)
        row = jnp.sum(p_own * gp_own, axis=0, keepdims=True) + jnp.sum(p_cross * gp_cross, axis=0, keepdims=True)
        ds_own = (p_own * (gp_own - row) * SCALE).astype(BF16)
        ds_cross = (p_cross * (gp_cross - row) * SCALE).astype(BF16)
        grad = dot_tn(ds_own, k) + dot_tn(ds_cross, k_cross)
        out_ref[:, rows, cols] = grad.astype(BF16).reshape(frames, GROUP, HEAD)
        for j, stat in enumerate((top, total, row)):
            stats_ref[i, 3 * h + j : 3 * h + j + 1] = stat


def key_kernel(side_ref, q_ref, kv_ref, q_recv_ref, g_ref, g_recv_ref, stats_ref, stats_recv_ref, gq_ref, out_ref):
    frames = q_ref.shape[0]
    shape = (frames, GROUP, HEAD)
    own_mask, cross_mask = masks(frames * GROUP, side_ref[0] == 0)
    for i, h, rows, cols in pieces(q_ref):
        k, v = take(kv_ref, 0, rows, cols), take(kv_ref, 1, rows, cols)
        grad_k, grad_v = 0.0, 0.0
        for mask, q, g, stats in (
            (own_mask, q_ref[:, rows, cols], g_ref[:, rows, cols], stats_ref),
            (cross_mask, q_recv_ref[:, rows, cols], g_recv_ref[:, rows, cols], stats_recv_ref),
        ):
            top, total, row = (stats[i, 3 * h + j : 3 * h + j + 1] for j in range(3))
            q, g = q.reshape(-1, HEAD), g.reshape(-1, HEAD)
            probs = jnp.where(mask, jnp.exp(scores_of(mask, k, q) - top) / total, 0.0)
            ds = (probs * (dot_nt(v, g) - row) * SCALE).astype(BF16)
            grad_k = grad_k + dot_nn(ds, q)
            grad_v = grad_v + dot_nn(probs.astype(BF16), g)
        out_ref[:, 3 * i, :, cols] = gq_ref[:, rows, cols]
        out_ref[:, 3 * i + 1, :, cols] = grad_k.astype(BF16).reshape(shape)
        out_ref[:, 3 * i + 2, :, cols] = grad_v.astype(BF16).reshape(shape)


def owner_columns(place_ref, offset, w_shape):
    width, parts = w_shape[0], w_shape[1] // w_shape[0]
    owner = lax.rem(place_ref[0] + offset + parts, parts)
    return pl.ds(pl.multiple_of(owner * width, width), width)


def attended_kernel(offsets, place_ref, w_ref, *refs):
    blocks, g_ref = refs[:-1], refs[-1]
    half = blocks[-1].shape[0]
    acc = 0.0
    for offset, ref in zip(offsets, blocks[:-2]):
        acc = acc + dot_nt(ref[...], w_ref[:, owner_columns(place_ref, offset, w_ref.shape)])
    last = w_ref[:, owner_columns(place_ref, len(offsets) // 2 + 1, w_ref.shape)]
    g_ref[:half] = (acc[:half] + dot_nt(blocks[-2][...], last)).astype(BF16)
    g_ref[half:] = (acc[half:] + dot_nt(blocks[-1][...], last)).astype(BF16)


def term_kernel(offsets, place_ref, att_ref, *refs):
    blocks, term_ref = refs[:-1], refs[-1]
    half = blocks[-1].shape[0]
    for offset, ref in zip(offsets, blocks[:-2]):
        term_ref[:, owner_columns(place_ref, offset, term_ref.shape)] = dot_tn(att_ref[...], ref[...]).astype(BF16)
    last = dot_tn(att_ref[:half], blocks[-2][...]) + dot_tn(att_ref[half:], blocks[-1][...])
    term_ref[:, owner_columns(place_ref, len(offsets) // 2 + 1, term_ref.shape)] = last.astype(BF16)


def per_group(kernel, name, flops, side, args, outs, vmem=32, out_specs=None):
    items = args[0].shape[-2]

    def spec(a):
        if a.dtype == F32:
            return pl.BlockSpec((STEP_GROUPS,) + a.shape[1:], lambda i: (i, 0, 0))
        block = a.shape[:-2] + (STEP_GROUPS * GROUP, a.shape[-1])
        lead = (0,) * (len(a.shape) - 2)
        return pl.BlockSpec(block, lambda i: lead + (i, 0))

    return pl.pallas_call(
        kernel,
        grid=(items // (STEP_GROUPS * GROUP),),
        in_specs=[SMEM] + [spec(a) for a in args],
        out_specs=out_specs or [spec(a) for a in outs],
        out_shape=[jax.ShapeDtypeStruct(a.shape, a.dtype) for a in outs],
        compiler_params=pltpu.CompilerParams(vmem_limit_bytes=vmem * 1024 * 1024),
        cost_estimate=pl.CostEstimate(flops=flops, bytes_accessed=4_000_000, transcendentals=400_000),
        name=name,
    )(side, *args)


def project(kernel, name, blocks, offsets, first, shape):
    vmem = pl.BlockSpec(memory_space=pltpu.VMEM)
    return pl.pallas_call(
        functools.partial(kernel, offsets),
        in_specs=[SMEM] + [vmem] * (1 + len(blocks)),
        out_specs=vmem,
        out_shape=jax.ShapeDtypeStruct(shape, BF16),
        compiler_params=PARAMS,
        cost_estimate=pl.CostEstimate(flops=800_000_000, bytes_accessed=4_500_000, transcendentals=0),
        name=name,
    )(lax.axis_index("tensor").reshape(1), first, *blocks)


def exchange(x, axes):
    return lax.all_to_all(x, axes, 0, 0, tiled=True)


def scatter_sum(x, axes):
    parts = exchange(x.reshape(lax.axis_size(axes), -1, x.shape[-1]), axes)
    return jnp.sum(parts.astype(F32), axis=0)


def shift(x, axis, by):
    size = lax.axis_size(axis)
    return lax.ppermute(x, axis, [(i, (i + by) % size) for i in range(size)])


def ring(x):
    size = lax.axis_size("tensor")
    half = x.shape[0] // 2
    blocks, offsets, up, down = [x], [0], x, x
    for step in range(1, size // 2):
        up, down = shift(up, "tensor", 1), shift(down, "tensor", -1)
        blocks += [up, down]
        offsets += [-step, step]
    blocks += [shift(up[:half], "tensor", 1), shift(down[half:], "tensor", -1)]
    return blocks, offsets


def gather(x, axes):
    copies = jnp.broadcast_to(x[None], (lax.axis_size(axes),) + x.shape)
    return exchange(copies, axes).reshape(-1, x.shape[-1])


def local(queries, keys, values, out_grad, out_proj):
    clips, _, patches, width = queries.shape
    near = lax.axis_size(NEAR)
    tokens = clips * patches
    items = tokens // near
    factor = 1.0 / math.sqrt(tokens * near * lax.axis_size("zh") * lax.axis_size("dp"))
    side = lax.axis_index("zh").astype(jnp.int32).reshape(1)
    queries, keys, values, out_grad = (a.reshape(near, items, width) for a in (queries, keys, values, out_grad))

    grad_own = exchange(out_grad, NEAR).reshape(tokens, width)
    qkv, grad_own = lax.optimization_barrier((jnp.stack([queries, keys, values], axis=1), grad_own))
    qkv = exchange(qkv, NEAR)
    q, kv = qkv[:, 0], qkv[:, 1:]
    kv_recv = lax.ppermute(kv, "zh", [(0, 1)])
    blocks, offsets = ring(grad_own)
    like = jax.ShapeDtypeStruct(q.shape, BF16)
    q_recv = lax.ppermute(q, "zh", [(1, 0)])
    g = project(attended_kernel, "grad_attended", blocks, offsets, out_proj, (tokens, width)).reshape(q.shape)
    g, kv_recv = lax.optimization_barrier((g, kv_recv))
    (att,) = per_group(attend_kernel, "attend", 400_000_000, side, [q, kv, kv_recv], [like], 8)
    term = project(term_kernel, "term", blocks, offsets, att.reshape(tokens, width), out_proj.shape)
    term, q_recv = lax.optimization_barrier((term, q_recv))
    g_recv = lax.ppermute(g, "zh", [(1, 0)])

    stats = jax.ShapeDtypeStruct((items // GROUP, 8, near * GROUP), F32)
    grad_q, stats = per_group(query_kernel, "grad_queries", 700_000_000, side, [q, kv, kv_recv, g], [like, stats], 8)

    total = scatter_sum(term, "x").astype(BF16)
    total = scatter_sum(total, "core").astype(BF16)
    total, g_recv, grad_q, stats = lax.optimization_barrier((total, g_recv, grad_q, stats))
    stats_recv = lax.ppermute(stats, "zh", [(1, 0)])
    total = (scatter_sum(total, ("zh", "dp")) * factor).astype(BF16)
    total, stats_recv = lax.optimization_barrier((total, stats_recv))
    args = [q, kv, q_recv, g, g_recv, stats, stats_recv, grad_q]
    groups, share = items // GROUP, out_proj.size // (near * GROUP * width)
    grads = jax.ShapeDtypeStruct((near, 3 * groups + share, GROUP, width), BF16)
    block = pl.BlockSpec((near, 3 * STEP_GROUPS, GROUP, width), lambda i: (0, i, 0, 0))
    (grads,) = per_group(key_kernel, "grad_keys_values", 1_000_000_000, side, args, [grads], 8, [block])
    total = gather(total, ("zh", "dp"))
    total, grads = lax.optimization_barrier((total, grads))
    copies = jnp.broadcast_to(total.reshape(1, share, GROUP, width), (near, share, GROUP, width))
    home = exchange(lax.dynamic_update_slice(grads, copies, (0, 3 * groups, 0, 0)), NEAR)
    grad_proj = home[:, 3 * groups :].reshape(out_proj.shape)
    grads = home[:, : 3 * groups].reshape(near, groups, 3, GROUP, width)
    return tuple(grads[:, :, j].reshape(clips, 1, patches, width) for j in range(3)) + (grad_proj,)


def solution(mesh):
    fine = Mesh(mesh.devices.reshape(2, 4, 2, 8, 4), ("zh", "x", "core", "tensor", "dp"))
    spec = P("dp", ("zh", "x", "core"), None, "tensor")
    return jax.shard_map(
        local,
        mesh=fine,
        in_specs=(spec, spec, spec, spec, P("tensor", None)),
        out_specs=(spec, spec, spec, P("tensor", None)),
        check_vma=False,
    )
```

```python
import functools
import math

import jax
import jax.numpy as jnp
from jax import lax
from jax.experimental import pallas as pl
from jax.experimental.pallas import tpu as pltpu
from jax.sharding import Mesh, PartitionSpec as P

HEAD = 128
SCALE = 1.0 / math.sqrt(HEAD)
MASKED = -1e30
GROUP = 16
STEP_GROUPS = 2
NEAR = ("x", "core")
BF16 = jnp.bfloat16
F32 = jnp.float32
SMEM = pl.BlockSpec(memory_space=pltpu.SMEM)
PARAMS = pltpu.CompilerParams(vmem_limit_bytes=16 * 1024 * 1024)


def dot(a, b, dims):
    return lax.dot_general(a, b, (dims, ((), ())), preferred_element_type=F32)


def dot_nt(a, b):
    return dot(a, b, ((1,), (1,)))


def dot_nn(a, b):
    return dot(a, b, ((1,), (0,)))


def dot_tn(a, b):
    return dot(a, b, ((0,), (0,)))


def masks(rows, crossing):
    key = lax.broadcasted_iota(jnp.int32, (rows, rows), 0)
    query = lax.broadcasted_iota(jnp.int32, (rows, rows), 1)
    own = (key % GROUP == query % GROUP) & (key // GROUP <= query // GROUP)
    cross = key % GROUP == query % GROUP + jnp.where(crossing, 0, GROUP)
    return own, cross


def scores_of(mask, keys, queries):
    return jnp.where(mask, dot_nt(keys, queries) * SCALE, MASKED)


def pieces(ref):
    for i in range(STEP_GROUPS):
        for h in range(ref.shape[-1] // HEAD):
            yield i, h, slice(i * GROUP, (i + 1) * GROUP), slice(h * HEAD, (h + 1) * HEAD)


def take(ref, j, rows, cols):
    return ref[:, j, rows, cols].reshape(-1, HEAD)


def softmax(q, k, k_cross, own_mask, cross_mask):
    s_own, s_cross = scores_of(own_mask, k, q), scores_of(cross_mask, k_cross, q)
    top = jnp.maximum(jnp.max(s_own, axis=0, keepdims=True), jnp.max(s_cross, axis=0, keepdims=True))
    e_own, e_cross = jnp.exp(s_own - top), jnp.exp(s_cross - top)
    total = jnp.sum(e_own, axis=0, keepdims=True) + jnp.sum(e_cross, axis=0, keepdims=True)
    return e_own / total, e_cross / total, top, total


def attend_kernel(side_ref, q_ref, kv_ref, recv_ref, att_ref):
    frames = q_ref.shape[0]
    own_mask, cross_mask = masks(frames * GROUP, side_ref[0] == 1)
    for _, _, rows, cols in pieces(q_ref):
        (k, v), (k_cross, v_cross) = ([take(ref, j, rows, cols) for j in range(2)] for ref in (kv_ref, recv_ref))
        q = q_ref[:, rows, cols].reshape(-1, HEAD)
        p_own, p_cross, _, _ = softmax(q, k, k_cross, own_mask, cross_mask)
        att = dot_tn(p_own.astype(BF16), v) + dot_tn(p_cross.astype(BF16), v_cross)
        att_ref[:, rows, cols] = att.astype(BF16).reshape(frames, GROUP, HEAD)


def query_kernel(side_ref, q_ref, kv_ref, recv_ref, g_ref, out_ref, stats_ref):
    frames = q_ref.shape[0]
    own_mask, cross_mask = masks(frames * GROUP, side_ref[0] == 1)
    for i, h, rows, cols in pieces(q_ref):
        (k, v), (k_cross, v_cross) = ([take(ref, j, rows, cols) for j in range(2)] for ref in (kv_ref, recv_ref))
        q = q_ref[:, rows, cols].reshape(-1, HEAD)
        p_own, p_cross, top, total = softmax(q, k, k_cross, own_mask, cross_mask)
        g = g_ref[:, rows, cols].reshape(-1, HEAD)
        gp_own, gp_cross = dot_nt(v, g), dot_nt(v_cross, g)
        row = jnp.sum(p_own * gp_own, axis=0, keepdims=True) + jnp.sum(p_cross * gp_cross, axis=0, keepdims=True)
        ds_own = (p_own * (gp_own - row) * SCALE).astype(BF16)
        ds_cross = (p_cross * (gp_cross - row) * SCALE).astype(BF16)
        grad = dot_tn(ds_own, k) + dot_tn(ds_cross, k_cross)
        out_ref[:, rows, cols] = grad.astype(BF16).reshape(frames, GROUP, HEAD)
        for j, stat in enumerate((top, total, row)):
            stats_ref[i, 3 * h + j : 3 * h + j + 1] = stat


def key_kernel(side_ref, q_ref, kv_ref, q_recv_ref, g_ref, g_recv_ref, stats_ref, stats_recv_ref, gq_ref, out_ref):
    frames = q_ref.shape[0]
    shape = (frames, GROUP, HEAD)
    own_mask, cross_mask = masks(frames * GROUP, side_ref[0] == 0)
    for i, h, rows, cols in pieces(q_ref):
        k, v = take(kv_ref, 0, rows, cols), take(kv_ref, 1, rows, cols)
        grad_k, grad_v = 0.0, 0.0
        for mask, q, g, stats in (
            (own_mask, q_ref[:, rows, cols], g_ref[:, rows, cols], stats_ref),
            (cross_mask, q_recv_ref[:, rows, cols], g_recv_ref[:, rows, cols], stats_recv_ref),
        ):
            top, total, row = (stats[i, 3 * h + j : 3 * h + j + 1] for j in range(3))
            q, g = q.reshape(-1, HEAD), g.reshape(-1, HEAD)
            probs = jnp.where(mask, jnp.exp(scores_of(mask, k, q) - top) / total, 0.0)
            ds = (probs * (dot_nt(v, g) - row) * SCALE).astype(BF16)
            grad_k = grad_k + dot_nn(ds, q)
            grad_v = grad_v + dot_nn(probs.astype(BF16), g)
        out_ref[:, 3 * i, :, cols] = gq_ref[:, rows, cols]
        out_ref[:, 3 * i + 1, :, cols] = grad_k.astype(BF16).reshape(shape)
        out_ref[:, 3 * i + 2, :, cols] = grad_v.astype(BF16).reshape(shape)


def owner_columns(place_ref, offset, w_shape):
    width, parts = w_shape[0], w_shape[1] // w_shape[0]
    owner = lax.rem(place_ref[0] + offset + parts, parts)
    return pl.ds(pl.multiple_of(owner * width, width), width)


def attended_kernel(offsets, place_ref, w_ref, *refs):
    blocks, g_ref = refs[:-1], refs[-1]
    half = blocks[-1].shape[0]
    acc = 0.0
    for offset, ref in zip(offsets, blocks[:-2]):
        acc = acc + dot_nt(ref[...], w_ref[:, owner_columns(place_ref, offset, w_ref.shape)])
    last = w_ref[:, owner_columns(place_ref, len(offsets) // 2 + 1, w_ref.shape)]
    g_ref[:half] = (acc[:half] + dot_nt(blocks[-2][...], last)).astype(BF16)
    g_ref[half:] = (acc[half:] + dot_nt(blocks[-1][...], last)).astype(BF16)


def term_kernel(offsets, place_ref, att_ref, *refs):
    blocks, term_ref = refs[:-1], refs[-1]
    half = blocks[-1].shape[0]
    for offset, ref in zip(offsets, blocks[:-2]):
        term_ref[:, owner_columns(place_ref, offset, term_ref.shape)] = dot_tn(att_ref[...], ref[...]).astype(BF16)
    last = dot_tn(att_ref[:half], blocks[-2][...]) + dot_tn(att_ref[half:], blocks[-1][...])
    term_ref[:, owner_columns(place_ref, len(offsets) // 2 + 1, term_ref.shape)] = last.astype(BF16)


def per_group(kernel, name, flops, side, args, outs, vmem=32, out_specs=None):
    items = args[0].shape[-2]

    def spec(a):
        if a.dtype == F32:
            return pl.BlockSpec((STEP_GROUPS,) + a.shape[1:], lambda i: (i, 0, 0))
        block = a.shape[:-2] + (STEP_GROUPS * GROUP, a.shape[-1])
        lead = (0,) * (len(a.shape) - 2)
        return pl.BlockSpec(block, lambda i: lead + (i, 0))

    return pl.pallas_call(
        kernel,
        grid=(items // (STEP_GROUPS * GROUP),),
        in_specs=[SMEM] + [spec(a) for a in args],
        out_specs=out_specs or [spec(a) for a in outs],
        out_shape=[jax.ShapeDtypeStruct(a.shape, a.dtype) for a in outs],
        compiler_params=pltpu.CompilerParams(vmem_limit_bytes=vmem * 1024 * 1024),
        cost_estimate=pl.CostEstimate(flops=flops, bytes_accessed=4_000_000, transcendentals=400_000),
        name=name,
    )(side, *args)


def project(kernel, name, blocks, offsets, first, shape):
    vmem = pl.BlockSpec(memory_space=pltpu.VMEM)
    return pl.pallas_call(
        functools.partial(kernel, offsets),
        in_specs=[SMEM] + [vmem] * (1 + len(blocks)),
        out_specs=vmem,
        out_shape=jax.ShapeDtypeStruct(shape, BF16),
        compiler_params=PARAMS,
        cost_estimate=pl.CostEstimate(flops=800_000_000, bytes_accessed=4_500_000, transcendentals=0),
        name=name,
    )(lax.axis_index("tensor").reshape(1), first, *blocks)


def exchange(x, axes):
    return lax.all_to_all(x, axes, 0, 0, tiled=True)


def scatter_sum(x, axes):
    parts = exchange(x.reshape(lax.axis_size(axes), -1, x.shape[-1]), axes)
    return jnp.sum(parts.astype(F32), axis=0)


def shift(x, axis, by):
    size = lax.axis_size(axis)
    return lax.ppermute(x, axis, [(i, (i + by) % size) for i in range(size)])


def ring(x):
    size = lax.axis_size("tensor")
    half = x.shape[0] // 2
    blocks, offsets, up, down = [x], [0], x, x
    for step in range(1, size // 2):
        up, down = shift(up, "tensor", 1), shift(down, "tensor", -1)
        blocks += [up, down]
        offsets += [-step, step]
    blocks += [shift(up[:half], "tensor", 1), shift(down[half:], "tensor", -1)]
    return blocks, offsets


def gather(x, axes):
    copies = jnp.broadcast_to(x[None], (lax.axis_size(axes),) + x.shape)
    return exchange(copies, axes).reshape(-1, x.shape[-1])


def local(queries, keys, values, out_grad, out_proj):
    clips, _, patches, width = queries.shape
    near = lax.axis_size(NEAR)
    tokens = clips * patches
    items = tokens // near
    factor = 1.0 / math.sqrt(tokens * near * lax.axis_size("zh") * lax.axis_size("dp"))
    side = lax.axis_index("zh").astype(jnp.int32).reshape(1)
    queries, keys, values, out_grad = (a.reshape(near, items, width) for a in (queries, keys, values, out_grad))

    grad_own = exchange(out_grad, NEAR).reshape(tokens, width)
    qkv, grad_own = lax.optimization_barrier((jnp.stack([queries, keys, values], axis=1), grad_own))
    qkv = exchange(qkv, NEAR)
    q, kv = qkv[:, 0], qkv[:, 1:]
    kv_recv = lax.ppermute(kv, "zh", [(0, 1)])
    blocks, offsets = ring(grad_own)
    like = jax.ShapeDtypeStruct(q.shape, BF16)
    q_recv = lax.ppermute(q, "zh", [(1, 0)])
    g = project(attended_kernel, "grad_attended", blocks, offsets, out_proj, (tokens, width)).reshape(q.shape)
    g, kv_recv = lax.optimization_barrier((g, kv_recv))
    (att,) = per_group(attend_kernel, "attend", 400_000_000, side, [q, kv, kv_recv], [like], 8)
    term = project(term_kernel, "term", blocks, offsets, att.reshape(tokens, width), out_proj.shape)
    term, q_recv = lax.optimization_barrier((term, q_recv))
    g_recv = lax.ppermute(g, "zh", [(1, 0)])

    stats = jax.ShapeDtypeStruct((items // GROUP, 8, near * GROUP), F32)
    grad_q, stats = per_group(query_kernel, "grad_queries", 700_000_000, side, [q, kv, kv_recv, g], [like, stats], 8)

    total = scatter_sum(term, NEAR).astype(BF16)
    total, g_recv, grad_q, stats = lax.optimization_barrier((total, g_recv, grad_q, stats))
    stats_recv = lax.ppermute(stats, "zh", [(1, 0)])
    total = (scatter_sum(total, ("zh", "dp")) * factor).astype(BF16)
    total, stats_recv = lax.optimization_barrier((total, stats_recv))
    args = [q, kv, q_recv, g, g_recv, stats, stats_recv, grad_q]
    groups, share = items // GROUP, out_proj.size // (near * GROUP * width)
    grads = jax.ShapeDtypeStruct((near, 3 * groups + share, GROUP, width), BF16)
    block = pl.BlockSpec((near, 3 * STEP_GROUPS, GROUP, width), lambda i: (0, i, 0, 0))
    (grads,) = per_group(key_kernel, "grad_keys_values", 1_000_000_000, side, args, [grads], 8, [block])
    total = gather(total, ("zh", "dp"))
    total, grads = lax.optimization_barrier((total, grads))
    copies = jnp.broadcast_to(total.reshape(1, share, GROUP, width), (near, share, GROUP, width))
    home = exchange(lax.dynamic_update_slice(grads, copies, (0, 3 * groups, 0, 0)), NEAR)
    grad_proj = home[:, 3 * groups :].reshape(out_proj.shape)
    grads = home[:, : 3 * groups].reshape(near, groups, 3, GROUP, width)
    return tuple(grads[:, :, j].reshape(clips, 1, patches, width) for j in range(3)) + (grad_proj,)


def solution(mesh):
    fine = Mesh(mesh.devices.reshape(2, 4, 2, 8, 4), ("zh", "x", "core", "tensor", "dp"))
    spec = P("dp", ("zh", "x", "core"), None, "tensor")
    return jax.shard_map(
        local,
        mesh=fine,
        in_specs=(spec, spec, spec, spec, P("tensor", None)),
        out_specs=(spec, spec, spec, P("tensor", None)),
        check_vma=False,
    )
```
